32 devices in a mesh: blk: 2 (over x), pair: 16 (over z, y, core).
Axes of the slice: x: 2, y: 2, z: 4, core: 2. Of those that a mesh axis runs over, the one named last changes fastest.
Arguments:
- panels: bfloat16 [96, 384, 1152], P('pair', None, 'blk'), may hold values from -1 to 1
- pattern: int32 [96, 2], P('pair', 'blk'), may hold values 0 or 1
- point_inverse: float32 [96, 9, 128], P('pair'), as said below
- camera_hessian: float32 [1152, 576], P('blk'), as said below
- damping: int32 [1152], P('blk'), may hold values from 0 to 3
- camera_grad: float32 [1152], P('blk'), may hold values from -6 to 6
- point_grad: float32 [96, 384], P('pair'), may hold values from -6 to 6
Outputs:
- schur: float32 [1152, 1152], P('pair', 'blk')
- reduced_rhs: float32 [1152], P('blk')
The draws below stay inside these ranges and needn't reach their ends.
Inputs may be any that keep to these rules, and one draw needn't show every extreme that they name: point_inverse is symmetric in its 3 x 3 entries with a positive diagonal. camera_hessian blocks are symmetric with a positive diagonal.
All inputs are finite; a program needn't handle non-finite values. No bound on the sum of `pattern` on one device may be relied on, other than what follows from the above.
Results may differ from the reference program's by a relative error of at most 0.003.
Values may be sent and summed in bfloat16 or wider, within the bound.
A program may use at most 128 MiB of HBM per device.

```python
import jax
import jax.numpy as jnp
from jax import lax

CAMW = 576
PTS = 128
NPB = 96
CAMS = 1152
N_BLK = 2


def draw_point_inverse(key, part):
    key_off = jax.random.fold_in(key, 11)
    key_diag = jax.random.fold_in(key, 12)
    off_raw = jax.random.uniform(key_off, (NPB, 3, 3, PTS), jnp.float32, -0.25, 0.25)
    diag_raw = jnp.exp(jax.random.uniform(key_diag, (NPB, 3, PTS), jnp.float32, jnp.log(0.5), jnp.log(2.0)))
    symmetric = 0.5 * (off_raw + jnp.swapaxes(off_raw, 1, 2))
    eye_mask = jnp.eye(3, dtype=jnp.float32)[None, :, :, None]
    full_matrix = symmetric * (1.0 - eye_mask) + eye_mask * diag_raw[:, :, None, :]
    return full_matrix.reshape(NPB, 9, PTS)


def draw_camera_hessian(key, part):
    key_off = jax.random.fold_in(key, 21)
    key_diag = jax.random.fold_in(key, 22)
    off_raw = 0.05 * jax.random.normal(key_off, (N_BLK, CAMW, CAMW), jnp.float32)
    diag_raw = jnp.exp(jax.random.uniform(key_diag, (N_BLK, CAMW), jnp.float32, 0.0, jnp.log(4.0)))
    symmetric = 0.5 * (off_raw + jnp.swapaxes(off_raw, 1, 2))
    eye_mask = jnp.eye(CAMW, dtype=jnp.float32)[None]
    full_matrix = symmetric * (1.0 - eye_mask) + eye_mask * diag_raw[:, :, None]
    return full_matrix.reshape(CAMS, CAMW)


def plant(entries, key, smallest, top_value):
    longest = entries.shape.index(max(entries.shape))
    spots = []
    for shift in (0, 1):
        where = [jax.random.randint(jax.random.fold_in(key, axis), (), 0, length) for axis, length in enumerate(entries.shape)]
        where[longest] = (where[longest] + shift) % entries.shape[longest]
        spots.append(tuple(where))
    return entries.at[spots[0]].set(smallest).at[spots[1]].set(top_value)


def level_of(own_key, dims, pieces, smallest, largest):
    gain = 1.0
    for dim, shards_of in pieces:
        draws = jax.random.uniform(jax.random.fold_in(jax.random.fold_in(own_key, 6), dim), (shards_of,), jnp.float32, smallest / len(pieces), largest / len(pieces))
        gain = gain * jnp.repeat(jnp.exp(draws), dims[dim] // shards_of).reshape((-1,) + (1,) * (len(dims) - 1 - dim))
    return gain


def bell_draw(rng, shape, width, limit, split=(), kind=jnp.bfloat16):
    entries = width * jax.random.normal(rng, shape, jnp.float32)
    if split:
        entries = entries * level_of(rng, shape, split, -0.22, 0.18)
    return jnp.clip(entries, -limit, limit).astype(kind)


def setup_inputs(seed: int = 0) -> dict:
    key_list = jax.random.split(jax.random.key(seed), 8)
    panels = bell_draw(key_list[0], (NPB, 3 * PTS, CAMS), ((3 * PTS * NPB) ** -0.25), 1.0, ((0, 16), (2, 2)))
    pattern = plant((jax.random.randint(key_list[1], (NPB, N_BLK), 0, 4) < 3).astype(jnp.int32), jax.random.fold_in(key_list[1], 1), 0, 1)
    point_inverse = draw_point_inverse(jax.random.fold_in(key_list[7], 71), 0)
    camera_hessian = draw_camera_hessian(jax.random.fold_in(key_list[7], 71), 0)
    damping = plant(jax.random.randint(key_list[4], (CAMS,), 0, 4), jax.random.fold_in(key_list[4], 1), 0, 3).astype(jnp.int32)
    camera_grad = bell_draw(key_list[5], (CAMS,), 1.0, 6.0, ((0, 2),), jnp.float32)
    point_grad = bell_draw(key_list[6], (NPB, 3 * PTS), 1.0, 6.0, ((0, 16),), jnp.float32)
    return {"panels": panels, "pattern": pattern, "point_inverse": point_inverse, "camera_hessian": camera_hessian, "damping": damping, "camera_grad": camera_grad, "point_grad": point_grad}


def apply_inverse(inverse, shaped):
    parts = []
    for row in range(3):
        total = inverse[:, row * 3, :, None] * shaped[:, 0]
        total = total + inverse[:, row * 3 + 1, :, None] * shaped[:, 1]
        total = total + inverse[:, row * 3 + 2, :, None] * shaped[:, 2]
        parts.append(total)
    return jnp.stack(parts, axis=1)


def reference(panels, pattern, point_inverse, camera_hessian, damping, camera_grad, point_grad):
    observed = jnp.repeat(pattern.astype(jnp.bfloat16), CAMW, axis=1)
    masked = panels * observed[:, None, :]
    shaped = masked.astype(jnp.float32).reshape(NPB, 3, PTS, CAMS)
    scaled = apply_inverse(point_inverse, shaped).astype(jnp.bfloat16).reshape(NPB * 3 * PTS, CAMS)
    flat_panels = masked.reshape(NPB * 3 * PTS, CAMS)
    product = lax.dot_general(scaled, flat_panels, (((0,), (0,)), ((), ())), preferred_element_type=jnp.float32)
    blocks = camera_hessian.reshape(N_BLK, CAMW, CAMW)
    diag_vals = jnp.diagonal(blocks, axis1=1, axis2=2)
    levels = 0.1 * jnp.power(2.0, damping.astype(jnp.float32)).reshape(N_BLK, CAMW)
    damped = blocks + jnp.eye(CAMW, dtype=jnp.float32)[None] * (levels * diag_vals)[:, :, None]
    block_eye = jnp.eye(N_BLK, dtype=jnp.float32)
    placed = block_eye[:, None, :, None] * damped[:, :, None, :]
    schur = placed.reshape(CAMS, CAMS) - product
    grads = point_grad.reshape(NPB, 3, PTS)
    point_step = apply_inverse(point_inverse, grads[:, :, :, None])[..., 0]
    point_step = point_step.astype(jnp.bfloat16).reshape(NPB * 3 * PTS)
    reduced_rhs = camera_grad - jnp.dot(point_step, flat_panels, preferred_element_type=jnp.float32)
    return schur, reduced_rhs
```

```python
import functools

import jax
import jax.numpy as jnp
import numpy as np
from jax import lax
from jax.experimental import pallas as pl
from jax.experimental.pallas import tpu as pltpu
from jax.sharding import PartitionSpec as P

MESH = pl.DeviceIdType.MESH
LANES = 128
F32 = jnp.float32
BF16 = jnp.bfloat16


def apply_inverse(inverse, shaped):
    parts = []
    for row in range(3):
        total = inverse[:, row * 3, :, None] * shaped[:, 0]
        total = total + inverse[:, row * 3 + 1, :, None] * shaped[:, 1]
        total = total + inverse[:, row * 3 + 2, :, None] * shaped[:, 2]
        parts.append(total)
    return jnp.stack(parts, axis=1)


def finish(piece, summed, camera_hessian, damping, camera_grad, own_rows):
    camera_width = camera_hessian.shape[1]
    row_start = lax.axis_index("pair") * own_rows
    first = row_start - lax.axis_index("blk") * camera_width
    inside = (first >= 0) & (first < camera_width)
    offset = jnp.clip(first, 0, camera_width - own_rows)
    rows = lax.dynamic_slice_in_dim(camera_hessian, offset, own_rows, 0)
    levels = 0.1 * lax.shift_left(jnp.ones_like(damping), damping).astype(F32)
    row_at = lax.broadcasted_iota(jnp.int32, rows.shape, 0) + offset
    col_at = lax.broadcasted_iota(jnp.int32, rows.shape, 1)
    damped = rows + jnp.where(row_at == col_at, levels[None, :] * rows, 0.0)
    schur = jnp.where(inside, damped, 0.0) - piece
    return schur, camera_grad - summed


def general_shards(panels, pattern, point_inverse, camera_hessian, damping, camera_grad, point_grad):
    block_count = panels.shape[0]
    camera_width = panels.shape[2]
    point_count = point_inverse.shape[2]
    panel_rows = block_count * 3 * point_count
    masked = panels * pattern.astype(BF16)[:, :, None]
    shaped = masked.astype(F32).reshape(block_count, 3, point_count, camera_width)
    scaled = apply_inverse(point_inverse, shaped).astype(BF16).reshape(panel_rows, camera_width)
    flat_panels = masked.reshape(panel_rows, camera_width)
    gathered = lax.all_gather(scaled, "blk", axis=1, tiled=True)
    own_rows = gathered.shape[1] // lax.axis_size("pair")
    piece = lax.psum_scatter(
        lax.dot_general(gathered, flat_panels, (((0,), (0,)), ((), ())), preferred_element_type=F32),
        "pair",
        scatter_dimension=0,
        tiled=True,
    )
    grads = point_grad.reshape(block_count, 3, point_count)
    point_step = apply_inverse(point_inverse, grads[:, :, :, None])[..., 0]
    point_step = point_step.astype(BF16).reshape(panel_rows)
    local_terms = jnp.dot(point_step, flat_panels, preferred_element_type=F32)
    summed = lax.psum(local_terms, "pair")
    return finish(piece, summed, camera_hessian, damping, camera_grad, own_rows)


def column_order(width, slabs, group):
    own = width // slabs
    full, rest = own // group, own % group
    hot = np.zeros((width, (full + 2) * LANES), np.float32)
    for c in range(full):
        for s in range(slabs):
            for r in range(group):
                hot[s * own + c * group + r, c * LANES + s * group + r] = 1
    for s in range(slabs):
        for r in range(rest):
            at = s * own + full * group + r
            hot[at, full * LANES + s * rest + r] = 1
            hot[at, (full + 1) * LANES + slabs * rest + s * rest + r] = 1
    return hot


class Names:
    def __init__(self):
        self.order, self.shapes = {}, []

    def add(self, name, shape):
        self.order[name] = len(self.shapes)
        self.shapes.append(shape)


def tdot(a, b):
    return lax.dot_general(a, b, (((0,), (0,)), ((), ())), preferred_element_type=F32)


def plan(nk, rows, width, slabs, own, group):
    full, rest = own // group, own % group
    stages = slabs.bit_length() - 1
    half = nk // 2 * rows
    names = Names()
    items = [[("d", own, width)]]
    for c in range(full):
        items.append([("t%d" % c, group, width), ("u%d" % c, own, LANES)])
    items.append([("t%d" % full, rest, width), ("u%d" % full, own, LANES)])
    copies = 0
    for item in items:
        for tag, r, w in item:
            n = slabs
            names.add(tag + "a0", pltpu.VMEM((n, r, w), F32))
            for i in range(stages):
                n //= 2
                names.add(tag + "s%d" % i, pltpu.VMEM((n * r, w), BF16))
                names.add(tag + "r%d" % i, pltpu.VMEM((n * r, w), BF16))
                names.add(tag + "a%d" % (i + 1), pltpu.VMEM((n, r, w), F32))
            names.add(tag + "s%d" % stages, pltpu.VMEM((r, w), BF16))
            names.add(tag + "r%d" % stages, pltpu.VMEM((r, w), BF16))
            if tag[0] == "u":
                names.add(tag + "sx", pltpu.VMEM((r, w), BF16))
                names.add(tag + "rx", pltpu.VMEM((r, w), BF16))
    for i in range(stages + 1):
        names.add("hs%d" % i, pltpu.VMEM((8, width), F32))
        names.add("hr%d" % i, pltpu.VMEM((8, width), F32))
    for c in range(full + 1):
        deep = half if c < full else half // 2
        names.add("xs%d" % c, pltpu.VMEM((deep, LANES), BF16))
        names.add("xr%d" % c, pltpu.VMEM((deep, LANES), BF16))
    names.add("scaled", pltpu.VMEM((nk, rows, width), BF16))
    names.add("mine", pltpu.VMEM((half, width), BF16))
    names.add("total", pltpu.VMEM((width, width), F32))
    count = len(names.shapes)
    names.add("send", pltpu.SemaphoreType.DMA((count,)))
    names.add("recv", pltpu.SemaphoreType.DMA((count,)))
    return names, items, stages, full, rest


def kernel(names, items, stages, full, rest, slabs, group, pattern, panels, inverse, grads, hot, piece, rhs, *refs):
    at = lambda name: refs[names.order[name]]
    nk, rows, width = panels.shape
    points = rows // 3
    half = nk // 2 * rows
    own = width // slabs
    blk = lax.axis_index("blk")
    pair = lax.axis_index("pair")
    bit = [lax.rem(lax.div(pair, 2**i), 2) for i in range(stages + 1)]
    mate = [{"pair": pair + (1 - 2 * bit[i]) * 2**i} for i in range(stages + 1)]
    across = {"blk": 1 - blk}
    top = bit[stages]
    owns_diag = top == blk
    owns_off = top != blk

    barrier = pltpu.get_barrier_semaphore()
    for other in mate + [across]:
        pl.semaphore_signal(barrier, inc=1, device_id=other, device_id_type=MESH)

    def copy(src, dst, other):
        n = names.order[src]
        return pltpu.make_async_remote_copy(
            src_ref=at(src),
            dst_ref=at(dst),
            send_sem=at("send").at[n],
            recv_sem=at("recv").at[n],
            device_id=other,
            device_id_type=MESH,
        )

    def xcopy(c):
        return copy("xs%d" % c, "xr%d" % c, across)

    def hop(tag, i):
        return copy(tag + "s%d" % i, tag + "r%d" % i, mate[i])

    def ucopy(tag):
        return copy(tag + "sx", tag + "rx", across)

    first = blk * (nk // 2)
    other_first = (1 - blk) * (nk // 2)
    for j in range(nk // 2):
        seen = pattern[first + j, 0].astype(F32)
        at("mine")[pl.ds(j * rows, rows), :] = (panels[first + j].astype(F32) * seen).astype(BF16)

    def fill(c):
        if c < full:
            columns = hot[:, pl.ds(c * LANES, LANES)]
            at("xs%d" % c)[...] = jnp.dot(at("mine")[...], columns, preferred_element_type=F32).astype(BF16)
        else:
            low = hot[:, pl.ds(full * LANES, LANES)]
            high = hot[:, pl.ds((full + 1) * LANES, LANES)]
            upper = at("mine")[pl.ds(0, half // 2), :]
            lower = at("mine")[pl.ds(half // 2, half // 2), :]
            packed = jnp.dot(upper, low, preferred_element_type=F32)
            packed = packed + jnp.dot(lower, high, preferred_element_type=F32)
            at("xs%d" % c)[...] = packed.astype(BF16)

    fill(0)
    pl.semaphore_wait(barrier, len(mate) + 1)
    xcopy(0).start()
    for c in range(1, full + 1):
        fill(c)
        if c == 1:
            xcopy(c).start()

    at("total")[...] = jnp.zeros((width, width), F32)
    at("hs0")[...] = jnp.zeros((8, width), F32)
    piece[...] = jnp.zeros_like(piece)

    def block(k, carry):
        seen = pattern[k, 0].astype(F32)
        masked = (panels[k].astype(F32) * seen).astype(BF16)
        wide = masked.astype(F32)
        flat = inverse[k]
        tall = jnp.concatenate([flat, jnp.zeros((16 - 9, points), F32)], axis=0).T
        picked = lax.broadcasted_iota(jnp.int32, grads.shape, 0) == k
        grad = jnp.sum(jnp.where(picked, grads[...], 0.0), axis=0, keepdims=True)
        parts, steps = [], []
        for a in range(3):
            total, step = None, None
            for c in range(3):
                n = a * 3 + c
                term = tall[:, n : n + 1] * wide[c * points : (c + 1) * points]
                part = flat[n : n + 1] * grad[:, c * points : (c + 1) * points]
                total = term if total is None else total + term
                step = part if step is None else step + part
            parts.append(total.astype(BF16))
            steps.append(step)
        for a in range(3):
            at("scaled")[k, pl.ds(a * points, points), :] = parts[a]
        at("total")[...] += tdot(at("scaled")[k], masked)
        stepped = jnp.broadcast_to(jnp.concatenate(steps, axis=1), (8, rows)).astype(BF16)
        at("hs0")[...] += jnp.dot(stepped, masked, preferred_element_type=F32)
        return carry

    lax.fori_loop(0, nk, block, 0)

    def held():
        return at("scaled")[pl.ds(other_first, nk // 2)].reshape(half, width)

    def produce(n):
        if n == 0:
            at("da0")[...] = at("total")[...].reshape(slabs, own, width)
            return
        c = n - 1
        xcopy(c).wait_recv()
        if c + 2 <= full:
            xcopy(c + 2).start()
        got = at("xr%d" % c)[...]
        mix = held()
        if c < full:
            at("t%da0" % c)[...] = tdot(got, mix).reshape(slabs, group, width)
            at("u%da0" % c)[...] = tdot(mix, got).reshape(slabs, own, LANES)
        else:
            packed = slabs * rest
            upper, lower = mix[: half // 2], mix[half // 2 :]
            both = tdot(got, upper)[:packed] + tdot(got, lower)[packed : 2 * packed]
            at("t%da0" % c)[...] = both.reshape(slabs, rest, width)
            lane = lax.broadcasted_iota(jnp.int32, (width, LANES), 1)
            side = jnp.where(lane < packed, tdot(upper, got), tdot(lower, got))
            at("u%da0" % c)[...] = side.reshape(slabs, own, LANES)

    def push(n, i):
        for tag, r, w in items[n]:
            acc = at(tag + "a%d" % i)
            if i < stages:
                count = slabs >> (i + 1)
                cast = [acc[2 * m + 1 - bit[i]].astype(BF16) for m in range(count)]
                for m in range(count):
                    at(tag + "s%d" % i)[pl.ds(m * r, r), :] = cast[m]
                hop(tag, i).start()
            else:
                at(tag + "s%d" % i)[...] = acc[0].astype(BF16)

                @pl.when(owns_diag if tag[0] == "t" else owns_off)
                def _():
                    hop(tag, i).start()
        if n == 0:
            hop("h", i).start()

    def pull(n, i):
        for tag, r, w in items[n]:
            acc = at(tag + "a%d" % i)
            if i < stages:
                hop(tag, i).wait_recv()
                for m in range(slabs >> (i + 1)):
                    got = at(tag + "r%d" % i)[pl.ds(m * r, r), :].astype(F32)
                    at(tag + "a%d" % (i + 1))[m] = acc[2 * m + bit[i]] + got
            else:

                @pl.when(owns_off if tag[0] == "t" else owns_diag)
                def _():
                    hop(tag, i).wait_recv()
                    both = acc[0] + at(tag + "r%d" % i)[...].astype(F32)
                    if tag[0] == "d":
                        piece[...] = both
                    elif tag[0] == "t":
                        piece[pl.ds((n - 1) * group, r), :] += both
                    else:
                        at(tag + "sx")[...] = both.astype(BF16)
                        ucopy(tag).start()
        if n == 0:
            hop("h", i).wait_recv()
            both = at("hs%d" % i)[...] + at("hr%d" % i)[...]
            if i < stages:
                at("hs%d" % (i + 1))[...] = both
            else:
                rhs[...] = both

    def place(n):
        tag = "u%d" % (n - 1)

        @pl.when(owns_off)
        def _():
            ucopy(tag).wait_recv()
            got = at(tag + "rx")[...]
            spots = [n - 1] if n - 1 < full else [full, full + 1]
            for g in spots:
                columns = hot[:, pl.ds(g * LANES, LANES)]
                piece[...] += lax.dot_general(
                    got, columns, (((1,), (1,)), ((), ())), preferred_element_type=F32
                )

    count = len(items)
    done = [-1] * count

    def advance(n):
        step = done[n] + 1
        if step == 0:
            produce(n)
            push(n, 0)
        elif step <= stages + 1:
            pull(n, step - 1)
            if step <= stages:
                push(n, step)
        elif step == stages + 2 and n > 0:
            place(n)
        else:
            return
        done[n] = step

    for n in range(count):
        for m in range(n):
            advance(m)
        advance(n)
        for m in range(n):
            advance(m)
    for _ in range(stages + 2):
        for m in range(count):
            advance(m)

    for c in range(full + 1):
        xcopy(c).wait_send()
    for item in items:
        for tag, r, w in item:
            for i in range(stages):
                hop(tag, i).wait_send()

            @pl.when(owns_diag if tag[0] == "t" else owns_off)
            def _():
                hop(tag, stages).wait_send()

            if tag[0] == "u":

                @pl.when(owns_diag)
                def _():
                    ucopy(tag).wait_send()

    for i in range(stages + 1):
        hop("h", i).wait_send()


def shards(panels, pattern, point_inverse, camera_hessian, damping, camera_grad, point_grad):
    nk, rows, width = panels.shape
    slabs = lax.axis_size("pair") // lax.axis_size("blk")
    own = width // slabs
    group = LANES // slabs
    names, items, stages, full, rest = plan(nk, rows, width, slabs, own, group)
    hot = jnp.asarray(column_order(width, slabs, group), BF16)
    vmem = pl.BlockSpec(memory_space=pltpu.VMEM)
    piece, rhs = pl.pallas_call(
        functools.partial(kernel, names, items, stages, full, rest, slabs, group),
        out_shape=(
            jax.ShapeDtypeStruct((own, width), F32),
            jax.ShapeDtypeStruct((8, width), F32),
        ),
        in_specs=[pl.BlockSpec(memory_space=pltpu.SMEM)] + [vmem] * 4,
        out_specs=(vmem, vmem),
        scratch_shapes=names.shapes,
        compiler_params=pltpu.CompilerParams(
            collective_id=0, has_side_effects=True, vmem_limit_bytes=50 * 2**20
        ),
    )(pattern, panels, point_inverse, point_grad, hot)
    return finish(piece, rhs[0], camera_hessian, damping, camera_grad, own)


def fits(mesh):
    pairs = mesh.shape["pair"]
    return mesh.shape["blk"] == 2 and pairs & (pairs - 1) == 0 and 4 <= pairs <= 32


def solution(mesh):
    def program(panels, pattern, point_inverse, camera_hessian, damping, camera_grad, point_grad):
        use = fits(mesh)
        if use:
            slabs = mesh.shape["pair"] // 2
            width = camera_hessian.shape[1]
            own, group = width // slabs, LANES // slabs
            use = (
                width % slabs == 0
                and own % 8 == 0
                and group % 8 == 0
                and own % group * slabs * 2 == LANES
                and panels.shape[0] // mesh.shape["pair"] % 2 == 0
                and point_inverse.shape[2] == LANES
            )
        return jax.shard_map(
            shards if use else general_shards,
            mesh=mesh,
            in_specs=(
                P("pair", None, "blk"),
                P("pair", "blk"),
                P("pair", None, None),
                P("blk", None),
                P("blk"),
                P("blk"),
                P("pair", None),
            ),
            out_specs=(P("pair", "blk"), P("blk")),
            check_vma=False,
        )(panels, pattern, point_inverse, camera_hessian, damping, camera_grad, point_grad)

    return program
```

```python
import functools

import jax
import jax.numpy as jnp
from jax import lax
from jax.experimental import pallas as pl
from jax.experimental.pallas import tpu as pltpu
from jax.sharding import PartitionSpec as P

MESH = pl.DeviceIdType.MESH
LANES = 128
F32 = jnp.float32
BF16 = jnp.bfloat16


def apply_inverse(inverse, shaped):
    parts = []
    for row in range(3):
        total = inverse[:, row * 3, :, None] * shaped[:, 0]
        total = total + inverse[:, row * 3 + 1, :, None] * shaped[:, 1]
        total = total + inverse[:, row * 3 + 2, :, None] * shaped[:, 2]
        parts.append(total)
    return jnp.stack(parts, axis=1)


def finish(piece, summed, camera_hessian, damping, camera_grad, own_rows):
    camera_width = camera_hessian.shape[1]
    row_start = lax.axis_index("pair") * own_rows
    first = row_start - lax.axis_index("blk") * camera_width
    inside = (first >= 0) & (first < camera_width)
    offset = jnp.clip(first, 0, camera_width - own_rows)
    rows = lax.dynamic_slice_in_dim(camera_hessian, offset, own_rows, 0)
    levels = 0.1 * lax.shift_left(jnp.ones_like(damping), damping).astype(F32)
    row_at = lax.broadcasted_iota(jnp.int32, rows.shape, 0) + offset
    col_at = lax.broadcasted_iota(jnp.int32, rows.shape, 1)
    damped = rows + jnp.where(row_at == col_at, levels[None, :] * rows, 0.0)
    schur = jnp.where(inside, damped, 0.0) - piece
    return schur, camera_grad - summed


def general_shards(panels, pattern, point_inverse, camera_hessian, damping, camera_grad, point_grad):
    block_count = panels.shape[0]
    camera_width = panels.shape[2]
    point_count = point_inverse.shape[2]
    panel_rows = block_count * 3 * point_count
    masked = panels * pattern.astype(BF16)[:, :, None]
    shaped = masked.astype(F32).reshape(block_count, 3, point_count, camera_width)
    scaled = apply_inverse(point_inverse, shaped).astype(BF16).reshape(panel_rows, camera_width)
    flat_panels = masked.reshape(panel_rows, camera_width)
    gathered = lax.all_gather(scaled, "blk", axis=1, tiled=True)
    own_rows = gathered.shape[1] // lax.axis_size("pair")
    piece = lax.psum_scatter(
        lax.dot_general(gathered, flat_panels, (((0,), (0,)), ((), ())), preferred_element_type=F32),
        "pair",
        scatter_dimension=0,
        tiled=True,
    )
    grads = point_grad.reshape(block_count, 3, point_count)
    point_step = apply_inverse(point_inverse, grads[:, :, :, None])[..., 0]
    point_step = point_step.astype(BF16).reshape(panel_rows)
    local_terms = jnp.dot(point_step, flat_panels, preferred_element_type=F32)
    summed = lax.psum(local_terms, "pair")
    return finish(piece, summed, camera_hessian, damping, camera_grad, own_rows)


class Names:
    def __init__(self):
        self.order, self.shapes = {}, []

    def add(self, name, shape):
        self.order[name] = len(self.shapes)
        self.shapes.append(shape)


def ndot(a, b):
    return lax.dot_general(a, b, (((1,), (1,)), ((), ())), preferred_element_type=F32)


def plan(nk, rows, width, slabs, own, group):
    sizes = [group] * (own // group)
    if own % group:
        sizes.append(own % group)
    stages = slabs.bit_length() - 1
    half = nk // 2 * rows
    names = Names()
    items = [[("d", own, width)]]
    for c, g in enumerate(sizes):
        items.append([("t%d" % c, g, width), ("u%d" % c, own, slabs * g)])
    for item in items:
        for tag, r, w in item:
            n = slabs
            names.add(tag + "a0", pltpu.VMEM((n, r, w), F32))
            for i in range(stages):
                n //= 2
                names.add(tag + "s%d" % i, pltpu.VMEM((n * r, w), BF16))
                names.add(tag + "r%d" % i, pltpu.VMEM((n * r, w), BF16))
                names.add(tag + "a%d" % (i + 1), pltpu.VMEM((n, r, w), F32))
            names.add(tag + "s%d" % stages, pltpu.VMEM((r, w), BF16))
            names.add(tag + "r%d" % stages, pltpu.VMEM((r, w), BF16))
            if tag[0] == "u":
                names.add(tag + "sx", pltpu.VMEM((r, w), BF16))
                names.add(tag + "rx", pltpu.VMEM((r, w), BF16))
    for i in range(stages + 1):
        names.add("hs%d" % i, pltpu.VMEM((8, width), F32))
        names.add("hr%d" % i, pltpu.VMEM((8, width), F32))
    for c, g in enumerate(sizes):
        names.add("xs%d" % c, pltpu.VMEM((slabs * g, half), BF16))
        names.add("xr%d" % c, pltpu.VMEM((slabs * g, half), BF16))
        names.add("hot%d" % c, pltpu.VMEM((width, slabs * g), BF16))
    names.add("raw", pltpu.VMEM((nk, width, rows), BF16))
    names.add("scaled", pltpu.VMEM((2, width, half), BF16))
    names.add("masked", pltpu.VMEM((2, width, half), BF16))
    count = len(names.shapes)
    names.add("send", pltpu.SemaphoreType.DMA((count,)))
    names.add("recv", pltpu.SemaphoreType.DMA((count,)))
    names.add("load", pltpu.SemaphoreType.DMA((nk,)))
    return names, items, stages, sizes


def kernel(names, items, stages, sizes, slabs, group, pattern, panels, inverse, grads, piece, rhs, *refs):
    at = lambda name: refs[names.order[name]]
    nk, width, rows = panels.shape
    points = rows // 3
    half = nk // 2 * rows
    own = width // slabs
    last = len(sizes) - 1
    blk = lax.axis_index("blk")
    pair = lax.axis_index("pair")
    bit = [lax.rem(lax.div(pair, 2**i), 2) for i in range(stages + 1)]
    mate = [{"pair": pair + (1 - 2 * bit[i]) * 2**i} for i in range(stages + 1)]
    across = {"blk": 1 - blk}
    top = bit[stages]
    owns_diag = top == blk
    owns_off = top != blk
    first = blk * (nk // 2)
    other_first = (1 - blk) * (nk // 2)
    order = [first + j for j in range(nk // 2)] + [other_first + j for j in range(nk // 2)]

    def load(m):
        return pltpu.make_async_copy(panels.at[order[m]], at("raw").at[order[m]], at("load").at[m])

    for m in range(nk):
        load(m).start()

    barrier = pltpu.get_barrier_semaphore()
    for other in mate + [across]:
        pl.semaphore_signal(barrier, inc=1, device_id=other, device_id_type=MESH)

    def copy(src, dst, other):
        n = names.order[src]
        return pltpu.make_async_remote_copy(
            src_ref=at(src),
            dst_ref=at(dst),
            send_sem=at("send").at[n],
            recv_sem=at("recv").at[n],
            device_id=other,
            device_id_type=MESH,
        )

    def xcopy(c):
        return copy("xs%d" % c, "xr%d" % c, across)

    def hop(tag, i):
        return copy(tag + "s%d" % i, tag + "r%d" % i, mate[i])

    def ucopy(tag):
        return copy(tag + "sx", tag + "rx", across)

    def pick(values, k):
        chosen = lax.broadcasted_iota(jnp.int32, values.shape, 0) == k
        return jnp.sum(jnp.where(chosen, values, 0.0), axis=0, keepdims=True)

    def observe(m):
        load(m).wait()
        k = order[m]
        wide = at("raw")[k].astype(F32) * pattern[0, k].astype(F32)
        lanes = pl.ds(m % (nk // 2) * rows, rows)
        at("masked")[m // (nk // 2), :, lanes] = wide.astype(BF16)
        if m < nk // 2:
            start = 0
            for c, g in enumerate(sizes):
                parts = [wide[s * own + start : s * own + start + g] for s in range(slabs)]
                at("xs%d" % c)[:, lanes] = jnp.concatenate(parts, axis=0).astype(BF16)
                start += g

    for m in range(nk // 2):
        observe(m)
    pl.semaphore_wait(barrier, len(mate) + 1)
    for c in range(min(3, len(sizes))):
        xcopy(c).start()
    for m in range(nk // 2, nk):
        observe(m)

    piece[...] = jnp.zeros_like(piece)
    flat = [inverse[n] for n in range(9)]
    terms = jnp.zeros((8, width), F32)
    for m in range(nk):
        side, lanes = m // (nk // 2), m % (nk // 2) * rows
        k = order[m]
        near = [pick(flat[n], k) for n in range(9)]
        grad = pick(grads[...], k)
        wide = [at("masked")[side, :, pl.ds(lanes + c * points, points)].astype(F32) for c in range(3)]
        steps = []
        for a in range(3):
            total, step = None, None
            for c in range(3):
                term = near[a * 3 + c] * wide[c]
                part = near[a * 3 + c] * grad[:, c * points : (c + 1) * points]
                total = term if total is None else total + term
                step = part if step is None else step + part
            at("scaled")[side, :, pl.ds(lanes + a * points, points)] = total.astype(BF16)
            steps.append(step)
        stepped = jnp.broadcast_to(jnp.concatenate(steps, axis=1), (8, rows)).astype(BF16)
        terms = terms + ndot(stepped, at("masked")[side, :, pl.ds(lanes, rows)])
    at("hs0")[...] = terms

    def produce(n):
        if n == 0:
            total = ndot(at("scaled")[0], at("masked")[0])
            total = total + ndot(at("scaled")[1], at("masked")[1])
            at("da0")[...] = total.reshape(slabs, own, width)
            return
        c, g = n - 1, sizes[n - 1]
        xcopy(c).wait_recv()
        if c + 3 <= last:
            xcopy(c + 3).start()
        got = at("xr%d" % c)[...]
        mix = at("scaled")[1]
        at("t%da0" % c)[...] = ndot(got, mix).reshape(slabs, g, width)
        at("u%da0" % c)[...] = ndot(mix, got).reshape(slabs, own, slabs * g)
        row = lax.broadcasted_iota(jnp.int32, (width, slabs * g), 0)
        lane = lax.broadcasted_iota(jnp.int32, (width, slabs * g), 1)
        shift = g.bit_length() - 1
        goal = lax.shift_right_logical(lane, shift) * own + c * group + (lane & (g - 1))
        at("hot%d" % c)[...] = jnp.where(row == goal, 1.0, 0.0).astype(BF16)

    def push(n, i):
        for tag, r, w in items[n]:
            acc = at(tag + "a%d" % i)
            if i < stages:
                count = slabs >> (i + 1)
                cast = [acc[2 * m + 1 - bit[i]].astype(BF16) for m in range(count)]
                for m in range(count):
                    at(tag + "s%d" % i)[pl.ds(m * r, r), :] = cast[m]
                hop(tag, i).start()
            else:
                at(tag + "s%d" % i)[...] = acc[0].astype(BF16)

                @pl.when(owns_diag if tag[0] == "t" else owns_off)
                def _():
                    hop(tag, i).start()
        if n == 0:
            hop("h", i).start()

    def pull(n, i):
        for tag, r, w in items[n]:
            acc = at(tag + "a%d" % i)
            if i < stages:
                hop(tag, i).wait_recv()
                for m in range(slabs >> (i + 1)):
                    got = at(tag + "r%d" % i)[pl.ds(m * r, r), :].astype(F32)
                    at(tag + "a%d" % (i + 1))[m] = acc[2 * m + bit[i]] + got
            else:

                @pl.when(owns_off if tag[0] == "t" else owns_diag)
                def _():
                    hop(tag, i).wait_recv()
                    both = acc[0] + at(tag + "r%d" % i)[...].astype(F32)
                    if tag[0] == "d":
                        piece[...] = both
                    elif tag[0] == "t":
                        piece[pl.ds((n - 1) * group, r), :] += both
                    else:
                        at(tag + "sx")[...] = both.astype(BF16)
                        ucopy(tag).start()
        if n == 0:
            hop("h", i).wait_recv()
            both = at("hs%d" % i)[...] + at("hr%d" % i)[...]
            if i < stages:
                at("hs%d" % (i + 1))[...] = both
            else:
                rhs[...] = both

    def place(n):
        tag = "u%d" % (n - 1)

        @pl.when(owns_off)
        def _():
            ucopy(tag).wait_recv()
            got = at(tag + "rx")[...]
            piece[...] += ndot(got, at("hot%d" % (n - 1))[...])

    count = len(items)
    done = [-1] * count

    def advance(n):
        step = done[n] + 1
        if step == 0:
            produce(n)
            push(n, 0)
        elif step <= stages + 1:
            pull(n, step - 1)
            if step <= stages:
                push(n, step)
        elif step == stages + 2 and n > 0:
            place(n)
        else:
            return
        done[n] = step

    for n in range(count):
        for m in range(n):
            advance(m)
        advance(n)
        for m in range(n):
            advance(m)
    for _ in range(stages + 2):
        for m in range(count):
            advance(m)

    for c in range(last + 1):
        xcopy(c).wait_send()
    for item in items:
        for tag, r, w in item:
            for i in range(stages):
                hop(tag, i).wait_send()

            @pl.when(owns_diag if tag[0] == "t" else owns_off)
            def _():
                hop(tag, stages).wait_send()

            if tag[0] == "u":

                @pl.when(owns_diag)
                def _():
                    ucopy(tag).wait_send()

    for i in range(stages + 1):
        hop("h", i).wait_send()


def shards(panels, pattern, point_inverse, camera_hessian, damping, camera_grad, point_grad):
    nk, rows, width = panels.shape
    slabs = lax.axis_size("pair") // lax.axis_size("blk")
    own = width // slabs
    group = LANES // slabs
    names, items, stages, sizes = plan(nk, rows, width, slabs, own, group)
    vmem = pl.BlockSpec(memory_space=pltpu.VMEM)
    piece, rhs = pl.pallas_call(
        functools.partial(kernel, names, items, stages, sizes, slabs, group),
        out_shape=(
            jax.ShapeDtypeStruct((own, width), F32),
            jax.ShapeDtypeStruct((8, width), F32),
        ),
        in_specs=[
            pl.BlockSpec(memory_space=pltpu.SMEM),
            pl.BlockSpec(memory_space=pl.ANY),
            vmem,
            vmem,
        ],
        out_specs=(vmem, vmem),
        scratch_shapes=names.shapes,
        compiler_params=pltpu.CompilerParams(
            collective_id=0, has_side_effects=True, vmem_limit_bytes=56 * 2**20
        ),
    )(pattern.T, jnp.swapaxes(panels, 1, 2), jnp.swapaxes(point_inverse, 0, 1), point_grad)
    return finish(piece, rhs[0], camera_hessian, damping, camera_grad, own)


def fits(mesh):
    pairs = mesh.shape["pair"]
    return mesh.shape["blk"] == 2 and pairs & (pairs - 1) == 0 and 4 <= pairs <= 32


def solution(mesh):
    def program(panels, pattern, point_inverse, camera_hessian, damping, camera_grad, point_grad):
        use = fits(mesh)
        if use:
            slabs = mesh.shape["pair"] // 2
            width = camera_hessian.shape[1]
            own, group = width // slabs, LANES // slabs
            use = (
                width % slabs == 0
                and own % 8 == 0
                and group % 8 == 0
                and own % group * slabs * 2 == LANES
                and panels.shape[0] // mesh.shape["pair"] % 2 == 0
                and point_inverse.shape[2] == LANES
            )
        return jax.shard_map(
            shards if use else general_shards,
            mesh=mesh,
            in_specs=(
                P("pair", None, "blk"),
                P("pair", "blk"),
                P("pair", None, None),
                P("blk", None),
                P("blk"),
                P("blk"),
                P("pair", None),
            ),
            out_specs=(P("pair", "blk"), P("blk")),
            check_vma=False,
        )(panels, pattern, point_inverse, camera_hessian, damping, camera_grad, point_grad)

    return program
```

```python
import functools

import jax
import jax.numpy as jnp
from jax import lax
from jax.experimental import pallas as pl
from jax.experimental.pallas import tpu as pltpu
from jax.sharding import PartitionSpec as P

MESH = pl.DeviceIdType.MESH
LANES = 128
F32 = jnp.float32
BF16 = jnp.bfloat16


def apply_inverse(inverse, shaped):
    parts = []
    for row in range(3):
        total = inverse[:, row * 3, :, None] * shaped[:, 0]
        total = total + inverse[:, row * 3 + 1, :, None] * shaped[:, 1]
        total = total + inverse[:, row * 3 + 2, :, None] * shaped[:, 2]
        parts.append(total)
    return jnp.stack(parts, axis=1)


def finish(piece, summed, camera_hessian, damping, camera_grad, own_rows):
    camera_width = camera_hessian.shape[1]
    row_start = lax.axis_index("pair") * own_rows
    first = row_start - lax.axis_index("blk") * camera_width
    inside = (first >= 0) & (first < camera_width)
    offset = jnp.clip(first, 0, camera_width - own_rows)
    rows = lax.dynamic_slice_in_dim(camera_hessian, offset, own_rows, 0)
    levels = 0.1 * lax.shift_left(jnp.ones_like(damping), damping).astype(F32)
    row_at = lax.broadcasted_iota(jnp.int32, rows.shape, 0) + offset
    col_at = lax.broadcasted_iota(jnp.int32, rows.shape, 1)
    damped = rows + jnp.where(row_at == col_at, levels[None, :] * rows, 0.0)
    schur = jnp.where(inside, damped, 0.0) - piece
    return schur, camera_grad - summed


def general_shards(panels, pattern, point_inverse, camera_hessian, damping, camera_grad, point_grad):
    block_count = panels.shape[0]
    camera_width = panels.shape[2]
    point_count = point_inverse.shape[2]
    panel_rows = block_count * 3 * point_count
    masked = panels * pattern.astype(BF16)[:, :, None]
    shaped = masked.astype(F32).reshape(block_count, 3, point_count, camera_width)
    scaled = apply_inverse(point_inverse, shaped).astype(BF16).reshape(panel_rows, camera_width)
    flat_panels = masked.reshape(panel_rows, camera_width)
    gathered = lax.all_gather(scaled, "blk", axis=1, tiled=True)
    own_rows = gathered.shape[1] // lax.axis_size("pair")
    piece = lax.psum_scatter(
        lax.dot_general(gathered, flat_panels, (((0,), (0,)), ((), ())), preferred_element_type=F32),
        "pair",
        scatter_dimension=0,
        tiled=True,
    )
    grads = point_grad.reshape(block_count, 3, point_count)
    point_step = apply_inverse(point_inverse, grads[:, :, :, None])[..., 0]
    point_step = point_step.astype(BF16).reshape(panel_rows)
    local_terms = jnp.dot(point_step, flat_panels, preferred_element_type=F32)
    summed = lax.psum(local_terms, "pair")
    return finish(piece, summed, camera_hessian, damping, camera_grad, own_rows)


class Names:
    def __init__(self):
        self.order, self.shapes = {}, []

    def add(self, name, shape):
        self.order[name] = len(self.shapes)
        self.shapes.append(shape)


def ndot(a, b):
    return lax.dot_general(a, b, (((1,), (1,)), ((), ())), preferred_element_type=F32)


def plan(nk, rows, width, slabs, own, group):
    sizes = [group] * (own // group)
    if own % group:
        sizes.append(own % group)
    stages = slabs.bit_length() - 1
    half = nk // 2 * rows
    names = Names()
    items = [[("d", own, width)]]
    for c, g in enumerate(sizes):
        items.append([("t%d" % c, g, width), ("u%d" % c, own, slabs * g)])
    for item in items:
        for tag, r, w in item:
            n = slabs
            names.add(tag + "a0", pltpu.VMEM((n, r, w), F32))
            for i in range(stages if tag == "d" else 1):
                n //= 2
                names.add(tag + "s%d" % i, pltpu.VMEM((n * r, w), BF16))
                names.add(tag + "r%d" % i, pltpu.VMEM((n * r, w), BF16))
                names.add(tag + "a%d" % (i + 1), pltpu.VMEM((n, r, w), F32))
            if tag == "d":
                names.add(tag + "s%d" % stages, pltpu.VMEM((r, w), BF16))
                names.add(tag + "r%d" % stages, pltpu.VMEM((r, w), BF16))
            else:
                names.add(tag + "out", pltpu.VMEM((slabs // 2, r, w), BF16))
                names.add(tag + "in", pltpu.VMEM((slabs, r, w), BF16))
                names.add(tag + "send", pltpu.SemaphoreType.DMA((slabs // 2,)))
                names.add(tag + "recv", pltpu.SemaphoreType.DMA((slabs,)))
            if tag[0] == "u":
                names.add(tag + "sx", pltpu.VMEM((r, w), BF16))
                names.add(tag + "rx", pltpu.VMEM((r, w), BF16))
    for i in range(stages + 1):
        names.add("hs%d" % i, pltpu.VMEM((8, width), F32))
        names.add("hr%d" % i, pltpu.VMEM((8, width), F32))
    for c, g in enumerate(sizes):
        names.add("xs%d" % c, pltpu.VMEM((slabs * g, half), BF16))
        names.add("xr%d" % c, pltpu.VMEM((slabs * g, half), BF16))
        names.add("hot%d" % c, pltpu.VMEM((width, slabs * g), BF16))
    names.add("raw", pltpu.VMEM((nk, width, rows), BF16))
    names.add("scaled", pltpu.VMEM((2, width, half), BF16))
    names.add("masked", pltpu.VMEM((2, width, half), BF16))
    count = len(names.shapes)
    names.add("send", pltpu.SemaphoreType.DMA((count,)))
    names.add("recv", pltpu.SemaphoreType.DMA((count,)))
    names.add("load", pltpu.SemaphoreType.DMA((nk,)))
    return names, items, stages, sizes


def kernel(names, items, stages, sizes, slabs, group, pattern, panels, inverse, grads, piece, rhs, *refs):
    at = lambda name: refs[names.order[name]]
    nk, width, rows = panels.shape
    points = rows // 3
    half = nk // 2 * rows
    own = width // slabs
    last = len(sizes) - 1
    blk = lax.axis_index("blk")
    pair = lax.axis_index("pair")
    bit = [lax.rem(lax.div(pair, 2**i), 2) for i in range(stages + 1)]
    mate = [{"pair": pair + (1 - 2 * bit[i]) * 2**i} for i in range(stages + 1)]
    across = {"blk": 1 - blk}
    top = bit[stages]
    owns_diag = top == blk
    owns_off = top != blk
    first = blk * (nk // 2)
    other_first = (1 - blk) * (nk // 2)
    order = [first + j for j in range(nk // 2)] + [other_first + j for j in range(nk // 2)]

    def load(m):
        return pltpu.make_async_copy(panels.at[order[m]], at("raw").at[order[m]], at("load").at[m])

    for m in range(nk):
        load(m).start()

    barrier = pltpu.get_barrier_semaphore()
    place_here = lax.div(pair, 2)
    for step in range(1, slabs):
        peer = {"pair": lax.rem(place_here + step, slabs) * 2 + bit[0]}
        pl.semaphore_signal(barrier, inc=1, device_id=peer, device_id_type=MESH)
    for other in [mate[0], across]:
        pl.semaphore_signal(barrier, inc=1, device_id=other, device_id_type=MESH)

    def copy(src, dst, other):
        n = names.order[src]
        return pltpu.make_async_remote_copy(
            src_ref=at(src),
            dst_ref=at(dst),
            send_sem=at("send").at[n],
            recv_sem=at("recv").at[n],
            device_id=other,
            device_id_type=MESH,
        )

    def xcopy(c):
        return copy("xs%d" % c, "xr%d" % c, across)

    def hop(tag, i):
        return copy(tag + "s%d" % i, tag + "r%d" % i, mate[i])

    def owner(tag, q):
        side = 1 - blk if tag[0] == "t" else blk
        return side * slabs + q * 2 + bit[0]

    def direct(tag, q):
        return pltpu.make_async_remote_copy(
            src_ref=at(tag + "out").at[q],
            dst_ref=at(tag + "in").at[place_here],
            send_sem=at(tag + "send").at[q],
            recv_sem=at(tag + "recv").at[place_here],
            device_id={"pair": owner(tag, q)},
            device_id_type=MESH,
        )

    def arrival(tag, j):
        return pltpu.make_async_remote_copy(
            src_ref=at(tag + "out").at[0],
            dst_ref=at(tag + "in").at[j],
            send_sem=at(tag + "send").at[0],
            recv_sem=at(tag + "recv").at[j],
            device_id=mate[0],
            device_id_type=MESH,
        )

    def ucopy(tag):
        return copy(tag + "sx", tag + "rx", across)

    def pick(values, k):
        chosen = lax.broadcasted_iota(jnp.int32, values.shape, 0) == k
        return jnp.sum(jnp.where(chosen, values, 0.0), axis=0, keepdims=True)

    def observe(m):
        load(m).wait()
        k = order[m]
        wide = at("raw")[k].astype(F32) * pattern[0, k].astype(F32)
        lanes = pl.ds(m % (nk // 2) * rows, rows)
        at("masked")[m // (nk // 2), :, lanes] = wide.astype(BF16)
        if m < nk // 2:
            start = 0
            for c, g in enumerate(sizes):
                parts = [wide[s * own + start : s * own + start + g] for s in range(slabs)]
                at("xs%d" % c)[:, lanes] = jnp.concatenate(parts, axis=0).astype(BF16)
                start += g

    for m in range(nk // 2):
        observe(m)
    pl.semaphore_wait(barrier, slabs + 1)
    for c in range(min(3, len(sizes))):
        xcopy(c).start()
    for m in range(nk // 2, nk):
        observe(m)

    piece[...] = jnp.zeros_like(piece)
    flat = [inverse[n] for n in range(9)]
    terms = jnp.zeros((8, width), F32)
    for m in range(nk):
        side, lanes = m // (nk // 2), m % (nk // 2) * rows
        k = order[m]
        near = [pick(flat[n], k) for n in range(9)]
        grad = pick(grads[...], k)
        wide = [at("masked")[side, :, pl.ds(lanes + c * points, points)].astype(F32) for c in range(3)]
        steps = []
        for a in range(3):
            total, step = None, None
            for c in range(3):
                term = near[a * 3 + c] * wide[c]
                part = near[a * 3 + c] * grad[:, c * points : (c + 1) * points]
                total = term if total is None else total + term
                step = part if step is None else step + part
            at("scaled")[side, :, pl.ds(lanes + a * points, points)] = total.astype(BF16)
            steps.append(step)
        stepped = jnp.broadcast_to(jnp.concatenate(steps, axis=1), (8, rows)).astype(BF16)
        terms = terms + ndot(stepped, at("masked")[side, :, pl.ds(lanes, rows)])
    at("hs0")[...] = terms

    def produce(n):
        if n == 0:
            total = ndot(at("scaled")[0], at("masked")[0])
            total = total + ndot(at("scaled")[1], at("masked")[1])
            at("da0")[...] = total.reshape(slabs, own, width)
            return
        c, g = n - 1, sizes[n - 1]
        xcopy(c).wait_recv()
        if c + 3 <= last:
            xcopy(c + 3).start()
        got = at("xr%d" % c)[...]
        mix = at("scaled")[1]
        at("t%da0" % c)[...] = ndot(got, mix).reshape(slabs, g, width)
        at("u%da0" % c)[...] = ndot(mix, got).reshape(slabs, own, slabs * g)
        row = lax.broadcasted_iota(jnp.int32, (width, slabs * g), 0)
        lane = lax.broadcasted_iota(jnp.int32, (width, slabs * g), 1)
        shift = g.bit_length() - 1
        goal = lax.shift_right_logical(lane, shift) * own + c * group + (lane & (g - 1))
        at("hot%d" % c)[...] = jnp.where(row == goal, 1.0, 0.0).astype(BF16)

    def push(n, i):
        for tag, r, w in items[n]:
            acc = at(tag + "a%d" % i)
            if i < stages:
                count = slabs >> (i + 1)
                for m in range(count):
                    at(tag + "s%d" % i)[pl.ds(m * r, r), :] = acc[2 * m + 1 - bit[i]].astype(BF16)
                hop(tag, i).start()
            else:
                at(tag + "s%d" % i)[...] = acc[0].astype(BF16)

                @pl.when(owns_off)
                def _():
                    hop(tag, i).start()
        if n == 0:
            hop("h", i).start()

    def pull(n, i):
        for tag, r, w in items[n]:
            acc = at(tag + "a%d" % i)
            if i < stages:
                hop(tag, i).wait_recv()
                for m in range(slabs >> (i + 1)):
                    got = at(tag + "r%d" % i)[pl.ds(m * r, r), :].astype(F32)
                    at(tag + "a%d" % (i + 1))[m] = acc[2 * m + bit[i]] + got
            else:

                @pl.when(owns_diag)
                def _():
                    hop(tag, i).wait_recv()
                    piece[...] = acc[0] + at(tag + "r%d" % i)[...].astype(F32)
        if n == 0:
            hop("h", i).wait_recv()
            both = at("hs%d" % i)[...] + at("hr%d" % i)[...]
            if i < stages:
                at("hs%d" % (i + 1))[...] = both
            else:
                rhs[...] = both

    def scatter(n):
        for tag, r, w in items[n]:
            for q in range(slabs // 2):
                cast = at(tag + "a1")[q].astype(BF16)
                at(tag + "out")[q] = cast
                here = owner(tag, q) == pair

                @pl.when(here)
                def _():
                    at(tag + "in")[place_here] = cast

                @pl.when(jnp.logical_not(here))
                def _():
                    direct(tag, q).start()

    def collect(n):
        for tag, r, w in items[n]:

            @pl.when(owns_off if tag[0] == "t" else owns_diag)
            def _():
                for j in range(slabs):

                    @pl.when(place_here != j)
                    def _():
                        arrival(tag, j).wait_recv()

                total = at(tag + "in")[0].astype(F32)
                for j in range(1, slabs):
                    total = total + at(tag + "in")[j].astype(F32)
                if tag[0] == "t":
                    piece[pl.ds((n - 1) * group, r), :] += total
                else:
                    at(tag + "sx")[...] = total.astype(BF16)
                    ucopy(tag).start()

    def place(n):
        tag = "u%d" % (n - 1)

        @pl.when(owns_off)
        def _():
            ucopy(tag).wait_recv()
            got = at(tag + "rx")[...]
            piece[...] += ndot(got, at("hot%d" % (n - 1))[...])

    count = len(items)
    done = [-1] * count

    def advance(n):
        step = done[n] + 1
        if step == 0:
            produce(n)
            push(n, 0)
        elif n == 0 and step <= stages + 1:
            pull(n, step - 1)
            if step <= stages:
                push(n, step)
        elif n > 0 and step == 1:
            pull(n, 0)
            scatter(n)
        elif n > 0 and step == 2:
            collect(n)
        elif n > 0 and step == 3:
            place(n)
        else:
            return
        done[n] = step

    for n in range(count):
        advance(n)
        for m in range(n):
            advance(m)
    for _ in range(3):
        for m in range(count):
            advance(m)
    assert done == [stages + 1] + [3] * (count - 1)

    for c in range(last + 1):
        xcopy(c).wait_send()
    for item in items:
        for tag, r, w in item:
            for i in range(stages if tag == "d" else 1):
                hop(tag, i).wait_send()
            if tag == "d":

                @pl.when(owns_off)
                def _():
                    hop(tag, stages).wait_send()
            else:
                for q in range(slabs // 2):

                    @pl.when(owner(tag, q) != pair)
                    def _():
                        direct(tag, q).wait_send()

            if tag[0] == "u":

                @pl.when(owns_diag)
                def _():
                    ucopy(tag).wait_send()

    for i in range(stages + 1):
        hop("h", i).wait_send()


def shards(panels, pattern, point_inverse, camera_hessian, damping, camera_grad, point_grad):
    nk, rows, width = panels.shape
    slabs = lax.axis_size("pair") // lax.axis_size("blk")
    own = width // slabs
    group = LANES // slabs
    names, items, stages, sizes = plan(nk, rows, width, slabs, own, group)
    vmem = pl.BlockSpec(memory_space=pltpu.VMEM)
    piece, rhs = pl.pallas_call(
        functools.partial(kernel, names, items, stages, sizes, slabs, group),
        out_shape=(
            jax.ShapeDtypeStruct((own, width), F32),
            jax.ShapeDtypeStruct((8, width), F32),
        ),
        in_specs=[
            pl.BlockSpec(memory_space=pltpu.SMEM),
            pl.BlockSpec(memory_space=pl.ANY),
            vmem,
            vmem,
        ],
        out_specs=(vmem, vmem),
        scratch_shapes=names.shapes,
        compiler_params=pltpu.CompilerParams(
            collective_id=0, has_side_effects=True, vmem_limit_bytes=56 * 2**20
        ),
    )(pattern.T, jnp.swapaxes(panels, 1, 2), jnp.swapaxes(point_inverse, 0, 1), point_grad)
    return finish(piece, rhs[0], camera_hessian, damping, camera_grad, own)


def fits(mesh):
    pairs = mesh.shape["pair"]
    return mesh.shape["blk"] == 2 and pairs & (pairs - 1) == 0 and 4 <= pairs <= 32


def solution(mesh):
    def program(panels, pattern, point_inverse, camera_hessian, damping, camera_grad, point_grad):
        use = fits(mesh)
        if use:
            slabs = mesh.shape["pair"] // 2
            width = camera_hessian.shape[1]
            own, group = width // slabs, LANES // slabs
            use = (
                width % slabs == 0
                and own % 8 == 0
                and group % 8 == 0
                and own % group * slabs * 2 == LANES
                and panels.shape[0] // mesh.shape["pair"] % 2 == 0
                and point_inverse.shape[2] == LANES
            )
        return jax.shard_map(
            shards if use else general_shards,
            mesh=mesh,
            in_specs=(
                P("pair", None, "blk"),
                P("pair", "blk"),
                P("pair", None, None),
                P("blk", None),
                P("blk"),
                P("blk"),
                P("pair", None),
            ),
            out_specs=(P("pair", "blk"), P("blk")),
            check_vma=False,
        )(panels, pattern, point_inverse, camera_hessian, damping, camera_grad, point_grad)

    return program
```

```python
import functools

import jax
import jax.numpy as jnp
from jax import lax
from jax.experimental import pallas as pl
from jax.experimental.pallas import tpu as pltpu
from jax.sharding import PartitionSpec as P

MESH = pl.DeviceIdType.MESH
LANES = 128
F32 = jnp.float32
BF16 = jnp.bfloat16


def apply_inverse(inverse, shaped):
    parts = []
    for row in range(3):
        total = inverse[:, row * 3, :, None] * shaped[:, 0]
        total = total + inverse[:, row * 3 + 1, :, None] * shaped[:, 1]
        total = total + inverse[:, row * 3 + 2, :, None] * shaped[:, 2]
        parts.append(total)
    return jnp.stack(parts, axis=1)


def finish(piece, summed, camera_hessian, damping, camera_grad, own_rows):
    camera_width = camera_hessian.shape[1]
    row_start = lax.axis_index("pair") * own_rows
    first = row_start - lax.axis_index("blk") * camera_width
    inside = (first >= 0) & (first < camera_width)
    offset = jnp.clip(first, 0, camera_width - own_rows)
    rows = lax.dynamic_slice_in_dim(camera_hessian, offset, own_rows, 0)
    levels = 0.1 * lax.shift_left(jnp.ones_like(damping), damping).astype(F32)
    row_at = lax.broadcasted_iota(jnp.int32, rows.shape, 0) + offset
    col_at = lax.broadcasted_iota(jnp.int32, rows.shape, 1)
    damped = rows + jnp.where(row_at == col_at, levels[None, :] * rows, 0.0)
    schur = jnp.where(inside, damped, 0.0) - piece
    return schur, camera_grad - summed


def general_shards(panels, pattern, point_inverse, camera_hessian, damping, camera_grad, point_grad):
    block_count = panels.shape[0]
    camera_width = panels.shape[2]
    point_count = point_inverse.shape[2]
    panel_rows = block_count * 3 * point_count
    masked = panels * pattern.astype(BF16)[:, :, None]
    shaped = masked.astype(F32).reshape(block_count, 3, point_count, camera_width)
    scaled = apply_inverse(point_inverse, shaped).astype(BF16).reshape(panel_rows, camera_width)
    flat_panels = masked.reshape(panel_rows, camera_width)
    gathered = lax.all_gather(scaled, "blk", axis=1, tiled=True)
    own_rows = gathered.shape[1] // lax.axis_size("pair")
    piece = lax.psum_scatter(
        lax.dot_general(gathered, flat_panels, (((0,), (0,)), ((), ())), preferred_element_type=F32),
        "pair",
        scatter_dimension=0,
        tiled=True,
    )
    grads = point_grad.reshape(block_count, 3, point_count)
    point_step = apply_inverse(point_inverse, grads[:, :, :, None])[..., 0]
    point_step = point_step.astype(BF16).reshape(panel_rows)
    local_terms = jnp.dot(point_step, flat_panels, preferred_element_type=F32)
    summed = lax.psum(local_terms, "pair")
    return finish(piece, summed, camera_hessian, damping, camera_grad, own_rows)


class Names:
    def __init__(self):
        self.order, self.shapes = {}, []

    def add(self, name, shape):
        self.order[name] = len(self.shapes)
        self.shapes.append(shape)


def ndot(a, b):
    return lax.dot_general(a, b, (((1,), (1,)), ((), ())), preferred_element_type=F32)


def plan(nk, rows, width, slabs, own, group):
    sizes = [group] * (own // group)
    if own % group:
        sizes.append(own % group)
    stages = slabs.bit_length() - 1
    half = nk // 2 * rows
    names = Names()
    items = [[("d", own, width)]]
    for c, g in enumerate(sizes):
        items.append([("t%d" % c, g, width), ("u%d" % c, own, slabs * g)])
    for item in items:
        for tag, r, w in item:
            n = slabs
            names.add(tag + "a0", pltpu.VMEM((n, r, w), F32))
            for i in range(stages if tag == "d" else 1):
                n //= 2
                names.add(tag + "s%d" % i, pltpu.VMEM((n * r, w), BF16))
                names.add(tag + "r%d" % i, pltpu.VMEM((n * r, w), BF16))
                names.add(tag + "a%d" % (i + 1), pltpu.VMEM((n, r, w), F32))
            if tag == "d":
                names.add(tag + "s%d" % stages, pltpu.VMEM((r, w), BF16))
                names.add(tag + "r%d" % stages, pltpu.VMEM((r, w), BF16))
            else:
                names.add(tag + "out", pltpu.VMEM((slabs // 2, r, w), BF16))
                names.add(tag + "in", pltpu.VMEM((slabs, r, w), BF16))
                names.add(tag + "send", pltpu.SemaphoreType.DMA((slabs // 2,)))
                names.add(tag + "recv", pltpu.SemaphoreType.DMA((slabs,)))
            if tag[0] == "u":
                names.add(tag + "sx", pltpu.VMEM((r, w), BF16))
                names.add(tag + "rx", pltpu.VMEM((r, w), BF16))
    for i in range(stages + 1):
        names.add("hs%d" % i, pltpu.VMEM((8, width), F32))
        names.add("hr%d" % i, pltpu.VMEM((8, width), F32))
    for c, g in enumerate(sizes):
        names.add("xs%d" % c, pltpu.VMEM((slabs * g, half), BF16))
        names.add("xr%d" % c, pltpu.VMEM((slabs * g, half), BF16))
        names.add("hot%d" % c, pltpu.VMEM((width, slabs * g), BF16))
    names.add("raw", pltpu.VMEM((nk, width, rows), BF16))
    names.add("scaled", pltpu.VMEM((2, width, half), BF16))
    names.add("masked", pltpu.VMEM((2, width, half), BF16))
    count = len(names.shapes)
    names.add("send", pltpu.SemaphoreType.DMA((count,)))
    names.add("recv", pltpu.SemaphoreType.DMA((count,)))
    names.add("load", pltpu.SemaphoreType.DMA((nk,)))
    return names, items, stages, sizes


def kernel(names, items, stages, sizes, slabs, group, pattern, panels, inverse, grads, piece, rhs, *refs):
    at = lambda name: refs[names.order[name]]
    nk, width, rows = panels.shape
    points = rows // 3
    half = nk // 2 * rows
    own = width // slabs
    last = len(sizes) - 1
    blk = lax.axis_index("blk")
    pair = lax.axis_index("pair")
    bit = [lax.rem(lax.div(pair, 2**i), 2) for i in range(stages + 1)]
    mate = [{"pair": pair + (1 - 2 * bit[i]) * 2**i} for i in range(stages + 1)]
    across = {"blk": 1 - blk}
    top = bit[stages]
    owns_diag = top == blk
    owns_off = top != blk
    first = blk * (nk // 2)
    other_first = (1 - blk) * (nk // 2)
    order = [first + j for j in range(nk // 2)] + [other_first + j for j in range(nk // 2)]

    def load(m):
        return pltpu.make_async_copy(panels.at[order[m]], at("raw").at[order[m]], at("load").at[m])

    for m in range(nk):
        load(m).start()

    barrier = pltpu.get_barrier_semaphore()
    place_here = lax.div(pair, 2)
    for step in range(1, slabs):
        peer = {"pair": lax.rem(place_here + step, slabs) * 2 + bit[0]}
        pl.semaphore_signal(barrier, inc=1, device_id=peer, device_id_type=MESH)
    for other in [mate[0], across]:
        pl.semaphore_signal(barrier, inc=1, device_id=other, device_id_type=MESH)

    def copy(src, dst, other):
        n = names.order[src]
        return pltpu.make_async_remote_copy(
            src_ref=at(src),
            dst_ref=at(dst),
            send_sem=at("send").at[n],
            recv_sem=at("recv").at[n],
            device_id=other,
            device_id_type=MESH,
        )

    def xcopy(c):
        return copy("xs%d" % c, "xr%d" % c, across)

    def hop(tag, i):
        return copy(tag + "s%d" % i, tag + "r%d" % i, mate[i])

    def owner(tag, q):
        side = 1 - blk if tag[0] == "t" else blk
        return side * slabs + q * 2 + bit[0]

    def direct(tag, q):
        return pltpu.make_async_remote_copy(
            src_ref=at(tag + "out").at[q],
            dst_ref=at(tag + "in").at[place_here],
            send_sem=at(tag + "send").at[q],
            recv_sem=at(tag + "recv").at[place_here],
            device_id={"pair": owner(tag, q)},
            device_id_type=MESH,
        )

    def arrival(tag, j):
        return pltpu.make_async_remote_copy(
            src_ref=at(tag + "out").at[0],
            dst_ref=at(tag + "in").at[j],
            send_sem=at(tag + "send").at[0],
            recv_sem=at(tag + "recv").at[j],
            device_id=mate[0],
            device_id_type=MESH,
        )

    def ucopy(tag):
        return copy(tag + "sx", tag + "rx", across)

    def pick(values, k):
        chosen = lax.broadcasted_iota(jnp.int32, values.shape, 0) == k
        return jnp.sum(jnp.where(chosen, values, 0.0), axis=0, keepdims=True)

    def observe(m):
        load(m).wait()
        k = order[m]
        wide = at("raw")[k].astype(F32) * pattern[0, k].astype(F32)
        lanes = pl.ds(m % (nk // 2) * rows, rows)
        at("masked")[m // (nk // 2), :, lanes] = wide.astype(BF16)
        if m < nk // 2:
            start = 0
            for c, g in enumerate(sizes):
                parts = [wide[s * own + start : s * own + start + g] for s in range(slabs)]
                at("xs%d" % c)[:, lanes] = jnp.concatenate(parts, axis=0).astype(BF16)
                start += g

    for m in range(nk // 2):
        observe(m)
    pl.semaphore_wait(barrier, slabs + 1)
    for c in range(min(3, len(sizes))):
        xcopy(c).start()
    for m in range(nk // 2, nk):
        observe(m)

    piece[...] = jnp.zeros_like(piece)
    flat = [inverse[n] for n in range(9)]
    terms = jnp.zeros((8, width), F32)
    for m in range(nk):
        side, lanes = m // (nk // 2), m % (nk // 2) * rows
        k = order[m]
        near = [pick(flat[n], k) for n in range(9)]
        grad = pick(grads[...], k)
        wide = [at("masked")[side, :, pl.ds(lanes + c * points, points)].astype(F32) for c in range(3)]
        steps = []
        for a in range(3):
            total, step = None, None
            for c in range(3):
                term = near[a * 3 + c] * wide[c]
                part = near[a * 3 + c] * grad[:, c * points : (c + 1) * points]
                total = term if total is None else total + term
                step = part if step is None else step + part
            at("scaled")[side, :, pl.ds(lanes + a * points, points)] = total.astype(BF16)
            steps.append(step)
        stepped = jnp.broadcast_to(jnp.concatenate(steps, axis=1), (8, rows)).astype(BF16)
        terms = terms + ndot(stepped, at("masked")[side, :, pl.ds(lanes, rows)])
    at("hs0")[...] = terms

    def produce(n):
        if n == 0:
            total = ndot(at("scaled")[0], at("masked")[0])
            total = total + ndot(at("scaled")[1], at("masked")[1])
            at("da0")[...] = total.reshape(slabs, own, width)
            return
        c, g = n - 1, sizes[n - 1]
        xcopy(c).wait_recv()
        if c + 3 <= last:
            xcopy(c + 3).start()
        got = at("xr%d" % c)[...]
        mix = at("scaled")[1]
        cross = ndot(mix, got)
        at("u%da0" % c)[...] = cross.reshape(slabs, own, slabs * g)
        at("t%da0" % c)[...] = cross.T.reshape(slabs, g, width)

    def build_orders():
        for c, g in enumerate(sizes):
            row = lax.broadcasted_iota(jnp.int32, (width, slabs * g), 0)
            lane = lax.broadcasted_iota(jnp.int32, (width, slabs * g), 1)
            shift = g.bit_length() - 1
            goal = lax.shift_right_logical(lane, shift) * own + c * group + (lane & (g - 1))
            at("hot%d" % c)[...] = jnp.where(row == goal, 1.0, 0.0).astype(BF16)

    def push(n, i):
        for tag, r, w in items[n]:
            acc = at(tag + "a%d" % i)
            if i < stages:
                count = slabs >> (i + 1)
                for m in range(count):
                    at(tag + "s%d" % i)[pl.ds(m * r, r), :] = acc[2 * m + 1 - bit[i]].astype(BF16)
                hop(tag, i).start()
            else:
                at(tag + "s%d" % i)[...] = acc[0].astype(BF16)

                @pl.when(owns_off)
                def _():
                    hop(tag, i).start()
        if n == 0:
            hop("h", i).start()

    def pull(n, i):
        for tag, r, w in items[n]:
            acc = at(tag + "a%d" % i)
            if i < stages:
                hop(tag, i).wait_recv()
                for m in range(slabs >> (i + 1)):
                    got = at(tag + "r%d" % i)[pl.ds(m * r, r), :].astype(F32)
                    at(tag + "a%d" % (i + 1))[m] = acc[2 * m + bit[i]] + got
            else:

                @pl.when(owns_diag)
                def _():
                    hop(tag, i).wait_recv()
                    piece[...] = acc[0] + at(tag + "r%d" % i)[...].astype(F32)
        if n == 0:
            hop("h", i).wait_recv()
            both = at("hs%d" % i)[...] + at("hr%d" % i)[...]
            if i < stages:
                at("hs%d" % (i + 1))[...] = both
            else:
                rhs[...] = both

    def scatter(n):
        for tag, r, w in items[n]:
            for q in range(slabs // 2):
                cast = at(tag + "a1")[q].astype(BF16)
                at(tag + "out")[q] = cast
                here = owner(tag, q) == pair

                @pl.when(here)
                def _():
                    at(tag + "in")[place_here] = cast

                @pl.when(jnp.logical_not(here))
                def _():
                    direct(tag, q).start()

    def collect(n):
        for tag, r, w in items[n]:

            @pl.when(owns_off if tag[0] == "t" else owns_diag)
            def _():
                for j in range(slabs):

                    @pl.when(place_here != j)
                    def _():
                        arrival(tag, j).wait_recv()

                total = at(tag + "in")[0].astype(F32)
                for j in range(1, slabs):
                    total = total + at(tag + "in")[j].astype(F32)
                if tag[0] == "t":
                    piece[pl.ds((n - 1) * group, r), :] += total
                else:
                    at(tag + "sx")[...] = total.astype(BF16)
                    ucopy(tag).start()

    def place(n):
        tag = "u%d" % (n - 1)

        @pl.when(owns_off)
        def _():
            ucopy(tag).wait_recv()
            got = at(tag + "rx")[...]
            piece[...] += ndot(got, at("hot%d" % (n - 1))[...])

    count = len(items)
    done = [-1] * count

    def advance(n):
        step = done[n] + 1
        if step == 0:
            produce(n)
            push(n, 0)
            if n == 0:
                build_orders()
        elif n == 0 and step <= stages + 1:
            pull(n, step - 1)
            if step <= stages:
                push(n, step)
        elif n > 0 and step == 1:
            pull(n, 0)
            scatter(n)
        elif n > 0 and step == 2:
            collect(n)
        elif n > 0 and step == 3:
            place(n)
        else:
            return
        done[n] = step

    for n in range(count):
        advance(n)
        for m in range(n):
            advance(m)
    for _ in range(3):
        for m in range(count):
            advance(m)
    assert done == [stages + 1] + [3] * (count - 1)

    for c in range(last + 1):
        xcopy(c).wait_send()
    for item in items:
        for tag, r, w in item:
            for i in range(stages if tag == "d" else 1):
                hop(tag, i).wait_send()
            if tag == "d":

                @pl.when(owns_off)
                def _():
                    hop(tag, stages).wait_send()
            else:
                for q in range(slabs // 2):

                    @pl.when(owner(tag, q) != pair)
                    def _():
                        direct(tag, q).wait_send()

            if tag[0] == "u":

                @pl.when(owns_diag)
                def _():
                    ucopy(tag).wait_send()

    for i in range(stages + 1):
        hop("h", i).wait_send()


def shards(panels, pattern, point_inverse, camera_hessian, damping, camera_grad, point_grad):
    nk, rows, width = panels.shape
    slabs = lax.axis_size("pair") // lax.axis_size("blk")
    own = width // slabs
    group = LANES // slabs
    names, items, stages, sizes = plan(nk, rows, width, slabs, own, group)
    vmem = pl.BlockSpec(memory_space=pltpu.VMEM)
    piece, rhs = pl.pallas_call(
        functools.partial(kernel, names, items, stages, sizes, slabs, group),
        out_shape=(
            jax.ShapeDtypeStruct((own, width), F32),
            jax.ShapeDtypeStruct((8, width), F32),
        ),
        in_specs=[
            pl.BlockSpec(memory_space=pltpu.SMEM),
            pl.BlockSpec(memory_space=pl.ANY),
            vmem,
            vmem,
        ],
        out_specs=(vmem, vmem),
        scratch_shapes=names.shapes,
        compiler_params=pltpu.CompilerParams(
            collective_id=0, has_side_effects=True, vmem_limit_bytes=56 * 2**20
        ),
    )(pattern.T, jnp.swapaxes(panels, 1, 2), jnp.swapaxes(point_inverse, 0, 1), point_grad)
    return finish(piece, rhs[0], camera_hessian, damping, camera_grad, own)


def fits(mesh):
    pairs = mesh.shape["pair"]
    return mesh.shape["blk"] == 2 and pairs & (pairs - 1) == 0 and 4 <= pairs <= 32


def solution(mesh):
    def program(panels, pattern, point_inverse, camera_hessian, damping, camera_grad, point_grad):
        use = fits(mesh)
        if use:
            slabs = mesh.shape["pair"] // 2
            width = camera_hessian.shape[1]
            own, group = width // slabs, LANES // slabs
            use = (
                width % slabs == 0
                and own % 8 == 0
                and group % 8 == 0
                and own % group * slabs * 2 == LANES
                and panels.shape[0] // mesh.shape["pair"] % 2 == 0
                and point_inverse.shape[2] == LANES
            )
        return jax.shard_map(
            shards if use else general_shards,
            mesh=mesh,
            in_specs=(
                P("pair", None, "blk"),
                P("pair", "blk"),
                P("pair", None, None),
                P("blk", None),
                P("blk"),
                P("blk"),
                P("pair", None),
            ),
            out_specs=(P("pair", "blk"), P("blk")),
            check_vma=False,
        )(panels, pattern, point_inverse, camera_hessian, damping, camera_grad, point_grad)

    return program
```

```python
import functools

import jax
import jax.numpy as jnp
from jax import lax
from jax.experimental import pallas as pl
from jax.experimental.pallas import tpu as pltpu
from jax.sharding import PartitionSpec as P

MESH = pl.DeviceIdType.MESH
LANES = 128
F32 = jnp.float32
BF16 = jnp.bfloat16


def apply_inverse(inverse, shaped):
    parts = []
    for row in range(3):
        total = inverse[:, row * 3, :, None] * shaped[:, 0]
        total = total + inverse[:, row * 3 + 1, :, None] * shaped[:, 1]
        total = total + inverse[:, row * 3 + 2, :, None] * shaped[:, 2]
        parts.append(total)
    return jnp.stack(parts, axis=1)


def finish(piece, summed, camera_hessian, damping, camera_grad, own_rows):
    camera_width = camera_hessian.shape[1]
    row_start = lax.axis_index("pair") * own_rows
    first = row_start - lax.axis_index("blk") * camera_width
    inside = (first >= 0) & (first < camera_width)
    offset = jnp.clip(first, 0, camera_width - own_rows)
    rows = lax.dynamic_slice_in_dim(camera_hessian, offset, own_rows, 0)
    levels = 0.1 * lax.shift_left(jnp.ones_like(damping), damping).astype(F32)
    row_at = lax.broadcasted_iota(jnp.int32, rows.shape, 0) + offset
    col_at = lax.broadcasted_iota(jnp.int32, rows.shape, 1)
    damped = rows + jnp.where(row_at == col_at, levels[None, :] * rows, 0.0)
    schur = jnp.where(inside, damped, 0.0) - piece
    return schur, camera_grad - summed


def general_shards(panels, pattern, point_inverse, camera_hessian, damping, camera_grad, point_grad):
    block_count = panels.shape[0]
    camera_width = panels.shape[2]
    point_count = point_inverse.shape[2]
    panel_rows = block_count * 3 * point_count
    masked = panels * pattern.astype(BF16)[:, :, None]
    shaped = masked.astype(F32).reshape(block_count, 3, point_count, camera_width)
    scaled = apply_inverse(point_inverse, shaped).astype(BF16).reshape(panel_rows, camera_width)
    flat_panels = masked.reshape(panel_rows, camera_width)
    gathered = lax.all_gather(scaled, "blk", axis=1, tiled=True)
    own_rows = gathered.shape[1] // lax.axis_size("pair")
    piece = lax.psum_scatter(
        lax.dot_general(gathered, flat_panels, (((0,), (0,)), ((), ())), preferred_element_type=F32),
        "pair",
        scatter_dimension=0,
        tiled=True,
    )
    grads = point_grad.reshape(block_count, 3, point_count)
    point_step = apply_inverse(point_inverse, grads[:, :, :, None])[..., 0]
    point_step = point_step.astype(BF16).reshape(panel_rows)
    local_terms = jnp.dot(point_step, flat_panels, preferred_element_type=F32)
    summed = lax.psum(local_terms, "pair")
    return finish(piece, summed, camera_hessian, damping, camera_grad, own_rows)


class Names:
    def __init__(self):
        self.order, self.shapes = {}, []

    def add(self, name, shape):
        self.order[name] = len(self.shapes)
        self.shapes.append(shape)


def ndot(a, b):
    return lax.dot_general(a, b, (((1,), (1,)), ((), ())), preferred_element_type=F32)


def plan(nk, rows, width, slabs, own, group):
    sizes = [group] * (own // group)
    if own % group:
        sizes.append(own % group)
    stages = slabs.bit_length() - 1
    half = nk // 2 * rows
    names = Names()
    items = [[("d", own, width)]]
    for c, g in enumerate(sizes):
        items.append([("t%d" % c, g, width), ("u%d" % c, own, slabs * g)])
    for item in items:
        for tag, r, w in item:
            n = slabs
            names.add(tag + "a0", pltpu.VMEM((n, r, w), F32))
            for i in range(stages if tag == "d" else 1):
                n //= 2
                names.add(tag + "s%d" % i, pltpu.VMEM((n * r, w), BF16))
                names.add(tag + "r%d" % i, pltpu.VMEM((n * r, w), BF16))
                names.add(tag + "a%d" % (i + 1), pltpu.VMEM((n, r, w), F32))
            if tag == "d":
                names.add(tag + "s%d" % stages, pltpu.VMEM((r, w), BF16))
                names.add(tag + "r%d" % stages, pltpu.VMEM((r, w), BF16))
            else:
                names.add(tag + "out", pltpu.VMEM((slabs // 2, r, w), BF16))
                names.add(tag + "in", pltpu.VMEM((slabs, r, w), BF16))
                names.add(tag + "send", pltpu.SemaphoreType.DMA((slabs // 2,)))
                names.add(tag + "recv", pltpu.SemaphoreType.DMA((slabs,)))
            if tag[0] == "u":
                names.add(tag + "sx", pltpu.VMEM((r, w), BF16))
                names.add(tag + "rx", pltpu.VMEM((r, w), BF16))
    for i in range(stages + 1):
        names.add("hs%d" % i, pltpu.VMEM((8, width), F32))
        names.add("hr%d" % i, pltpu.VMEM((8, width), F32))
    for c, g in enumerate(sizes):
        names.add("xs%d" % c, pltpu.VMEM((slabs * g, half), BF16))
        names.add("xr%d" % c, pltpu.VMEM((slabs * g, half), BF16))
        names.add("hot%d" % c, pltpu.VMEM((width, slabs * g), BF16))
    names.add("raw", pltpu.VMEM((nk, width, rows), BF16))
    names.add("scaled", pltpu.VMEM((2, width, half), BF16))
    names.add("masked", pltpu.VMEM((2, width, half), BF16))
    count = len(names.shapes)
    names.add("send", pltpu.SemaphoreType.DMA((count,)))
    names.add("recv", pltpu.SemaphoreType.DMA((count,)))
    names.add("load", pltpu.SemaphoreType.DMA((nk,)))
    return names, items, stages, sizes


def kernel(names, items, stages, sizes, slabs, group, pattern, panels, inverse, grads, piece, rhs, *refs):
    at = lambda name: refs[names.order[name]]
    nk, width, rows = panels.shape
    points = rows // 3
    half = nk // 2 * rows
    own = width // slabs
    last = len(sizes) - 1
    blk = lax.axis_index("blk")
    pair = lax.axis_index("pair")
    bit = [lax.rem(lax.div(pair, 2**i), 2) for i in range(stages + 1)]
    mate = [{"pair": pair + (1 - 2 * bit[i]) * 2**i} for i in range(stages + 1)]
    across = {"blk": 1 - blk}
    top = bit[stages]
    owns_diag = top == blk
    owns_off = top != blk
    first = blk * (nk // 2)
    other_first = (1 - blk) * (nk // 2)
    order = [first + j for j in range(nk // 2)] + [other_first + j for j in range(nk // 2)]

    def load(m):
        return pltpu.make_async_copy(panels.at[order[m]], at("raw").at[order[m]], at("load").at[m])

    for m in range(nk):
        load(m).start()

    barrier = pltpu.get_barrier_semaphore()
    place_here = lax.div(pair, 2)
    for step in range(1, slabs):
        peer = {"pair": lax.rem(place_here + step, slabs) * 2 + bit[0]}
        pl.semaphore_signal(barrier, inc=1, device_id=peer, device_id_type=MESH)
    for other in [mate[0], across]:
        pl.semaphore_signal(barrier, inc=1, device_id=other, device_id_type=MESH)

    def copy(src, dst, other):
        n = names.order[src]
        return pltpu.make_async_remote_copy(
            src_ref=at(src),
            dst_ref=at(dst),
            send_sem=at("send").at[n],
            recv_sem=at("recv").at[n],
            device_id=other,
            device_id_type=MESH,
        )

    def xcopy(c):
        return copy("xs%d" % c, "xr%d" % c, across)

    def hop(tag, i):
        return copy(tag + "s%d" % i, tag + "r%d" % i, mate[i])

    def owner(tag, q):
        side = 1 - blk if tag[0] == "t" else blk
        return side * slabs + q * 2 + bit[0]

    def direct(tag, q):
        return pltpu.make_async_remote_copy(
            src_ref=at(tag + "out").at[q],
            dst_ref=at(tag + "in").at[place_here],
            send_sem=at(tag + "send").at[q],
            recv_sem=at(tag + "recv").at[place_here],
            device_id={"pair": owner(tag, q)},
            device_id_type=MESH,
        )

    def arrival(tag, j):
        return pltpu.make_async_remote_copy(
            src_ref=at(tag + "out").at[0],
            dst_ref=at(tag + "in").at[j],
            send_sem=at(tag + "send").at[0],
            recv_sem=at(tag + "recv").at[j],
            device_id=mate[0],
            device_id_type=MESH,
        )

    def ucopy(tag):
        return copy(tag + "sx", tag + "rx", across)

    def pick(values, k):
        chosen = lax.broadcasted_iota(jnp.int32, values.shape, 0) == k
        return jnp.sum(jnp.where(chosen, values, 0.0), axis=0, keepdims=True)

    def observe(m):
        load(m).wait()
        k = order[m]
        wide = at("raw")[k].astype(F32) * pattern[0, k].astype(F32)
        lanes = pl.ds(m % (nk // 2) * rows, rows)
        at("masked")[m // (nk // 2), :, lanes] = wide.astype(BF16)
        if m < nk // 2:
            start = 0
            for c, g in enumerate(sizes):
                parts = [wide[s * own + start : s * own + start + g] for s in range(slabs)]
                at("xs%d" % c)[:, lanes] = jnp.concatenate(parts, axis=0).astype(BF16)
                start += g

    for m in range(nk // 2):
        observe(m)
    pl.semaphore_wait(barrier, slabs + 1)
    for c in range(min(2, len(sizes))):
        xcopy(c).start()
    for m in range(nk // 2, nk):
        observe(m)

    piece[...] = jnp.zeros_like(piece)
    flat = [inverse[n] for n in range(9)]
    terms = jnp.zeros((8, width), F32)
    for m in range(nk):
        side, lanes = m // (nk // 2), m % (nk // 2) * rows
        k = order[m]
        near = [pick(flat[n], k) for n in range(9)]
        grad = pick(grads[...], k)
        wide = [at("masked")[side, :, pl.ds(lanes + c * points, points)].astype(F32) for c in range(3)]
        steps = []
        for a in range(3):
            total, step = None, None
            for c in range(3):
                term = near[a * 3 + c] * wide[c]
                part = near[a * 3 + c] * grad[:, c * points : (c + 1) * points]
                total = term if total is None else total + term
                step = part if step is None else step + part
            at("scaled")[side, :, pl.ds(lanes + a * points, points)] = total.astype(BF16)
            steps.append(step)
        stepped = jnp.broadcast_to(jnp.concatenate(steps, axis=1), (8, rows)).astype(BF16)
        terms = terms + ndot(stepped, at("masked")[side, :, pl.ds(lanes, rows)])
    at("hs0")[...] = terms

    def produce(n):
        if n == 0:
            total = ndot(at("scaled")[0], at("masked")[0])
            total = total + ndot(at("scaled")[1], at("masked")[1])
            at("da0")[...] = total.reshape(slabs, own, width)
            return
        c, g = n - 1, sizes[n - 1]
        xcopy(c).wait_recv()
        if c + 2 <= last:
            xcopy(c + 2).start()
        got = at("xr%d" % c)[...]
        mix = at("scaled")[1]
        cross = ndot(mix, got)
        at("u%da0" % c)[...] = cross.reshape(slabs, own, slabs * g)
        at("t%da0" % c)[...] = cross.T.reshape(slabs, g, width)

    def build_orders():
        for c, g in enumerate(sizes):
            row = lax.broadcasted_iota(jnp.int32, (width, slabs * g), 0)
            lane = lax.broadcasted_iota(jnp.int32, (width, slabs * g), 1)
            shift = g.bit_length() - 1
            goal = lax.shift_right_logical(lane, shift) * own + c * group + (lane & (g - 1))
            at("hot%d" % c)[...] = jnp.where(row == goal, 1.0, 0.0).astype(BF16)

    def push(n, i):
        for tag, r, w in items[n]:
            acc = at(tag + "a%d" % i)
            if i < stages:
                count = slabs >> (i + 1)
                for m in range(count):
                    at(tag + "s%d" % i)[pl.ds(m * r, r), :] = acc[2 * m + 1 - bit[i]].astype(BF16)
                hop(tag, i).start()
            else:
                at(tag + "s%d" % i)[...] = acc[0].astype(BF16)

                @pl.when(owns_off)
                def _():
                    hop(tag, i).start()
        if n == 0:
            hop("h", i).start()

    def pull(n, i):
        for tag, r, w in items[n]:
            acc = at(tag + "a%d" % i)
            if i < stages:
                hop(tag, i).wait_recv()
                for m in range(slabs >> (i + 1)):
                    got = at(tag + "r%d" % i)[pl.ds(m * r, r), :].astype(F32)
                    at(tag + "a%d" % (i + 1))[m] = acc[2 * m + bit[i]] + got
            else:

                @pl.when(owns_diag)
                def _():
                    hop(tag, i).wait_recv()
                    piece[...] = acc[0] + at(tag + "r%d" % i)[...].astype(F32)
        if n == 0:
            hop("h", i).wait_recv()
            both = at("hs%d" % i)[...] + at("hr%d" % i)[...]
            if i < stages:
                at("hs%d" % (i + 1))[...] = both
            else:
                rhs[...] = both

    def scatter(n):
        for tag, r, w in items[n]:
            for q in range(slabs // 2):
                cast = at(tag + "a1")[q].astype(BF16)
                at(tag + "out")[q] = cast
                here = owner(tag, q) == pair

                @pl.when(here)
                def _():
                    at(tag + "in")[place_here] = cast

                @pl.when(jnp.logical_not(here))
                def _():
                    direct(tag, q).start()

    def collect(n):
        for tag, r, w in items[n]:

            @pl.when(owns_off if tag[0] == "t" else owns_diag)
            def _():
                for j in range(slabs):

                    @pl.when(place_here != j)
                    def _():
                        arrival(tag, j).wait_recv()

                total = at(tag + "in")[0].astype(F32)
                for j in range(1, slabs):
                    total = total + at(tag + "in")[j].astype(F32)
                if tag[0] == "t":
                    piece[pl.ds((n - 1) * group, r), :] += total
                else:
                    at(tag + "sx")[...] = total.astype(BF16)
                    ucopy(tag).start()

    def place(n):
        tag = "u%d" % (n - 1)

        @pl.when(owns_off)
        def _():
            ucopy(tag).wait_recv()
            got = at(tag + "rx")[...]
            piece[...] += ndot(got, at("hot%d" % (n - 1))[...])

    count = len(items)
    done = [-1] * count

    def advance(n):
        step = done[n] + 1
        if step == 0:
            produce(n)
            push(n, 0)
            if n == 0:
                build_orders()
        elif n == 0 and step <= stages + 1:
            pull(n, step - 1)
            if step <= stages:
                push(n, step)
        elif n > 0 and step == 1:
            pull(n, 0)
            scatter(n)
        elif n > 0 and step == 2:
            collect(n)
        elif n > 0 and step == 3:
            place(n)
        else:
            return
        done[n] = step

    for n in range(count):
        advance(n)
        for m in range(n):
            advance(m)
    for _ in range(3):
        for m in range(count):
            advance(m)
    assert done == [stages + 1] + [3] * (count - 1)

    for c in range(last + 1):
        xcopy(c).wait_send()
    for item in items:
        for tag, r, w in item:
            for i in range(stages if tag == "d" else 1):
                hop(tag, i).wait_send()
            if tag == "d":

                @pl.when(owns_off)
                def _():
                    hop(tag, stages).wait_send()
            else:
                for q in range(slabs // 2):

                    @pl.when(owner(tag, q) != pair)
                    def _():
                        direct(tag, q).wait_send()

            if tag[0] == "u":

                @pl.when(owns_diag)
                def _():
                    ucopy(tag).wait_send()

    for i in range(stages + 1):
        hop("h", i).wait_send()


def shards(panels, pattern, point_inverse, camera_hessian, damping, camera_grad, point_grad):
    nk, rows, width = panels.shape
    slabs = lax.axis_size("pair") // lax.axis_size("blk")
    own = width // slabs
    group = LANES // slabs
    names, items, stages, sizes = plan(nk, rows, width, slabs, own, group)
    vmem = pl.BlockSpec(memory_space=pltpu.VMEM)
    piece, rhs = pl.pallas_call(
        functools.partial(kernel, names, items, stages, sizes, slabs, group),
        out_shape=(
            jax.ShapeDtypeStruct((own, width), F32),
            jax.ShapeDtypeStruct((8, width), F32),
        ),
        in_specs=[
            pl.BlockSpec(memory_space=pltpu.SMEM),
            pl.BlockSpec(memory_space=pl.ANY),
            vmem,
            vmem,
        ],
        out_specs=(vmem, vmem),
        scratch_shapes=names.shapes,
        compiler_params=pltpu.CompilerParams(
            collective_id=0, has_side_effects=True, vmem_limit_bytes=56 * 2**20
        ),
    )(pattern.T, jnp.swapaxes(panels, 1, 2), jnp.swapaxes(point_inverse, 0, 1), point_grad)
    return finish(piece, rhs[0], camera_hessian, damping, camera_grad, own)


def fits(mesh):
    pairs = mesh.shape["pair"]
    return mesh.shape["blk"] == 2 and pairs & (pairs - 1) == 0 and 4 <= pairs <= 32


def solution(mesh):
    def program(panels, pattern, point_inverse, camera_hessian, damping, camera_grad, point_grad):
        use = fits(mesh)
        if use:
            slabs = mesh.shape["pair"] // 2
            width = camera_hessian.shape[1]
            own, group = width // slabs, LANES // slabs
            use = (
                width % slabs == 0
                and own % 8 == 0
                and group % 8 == 0
                and own % group * slabs * 2 == LANES
                and panels.shape[0] // mesh.shape["pair"] % 2 == 0
                and point_inverse.shape[2] == LANES
            )
        return jax.shard_map(
            shards if use else general_shards,
            mesh=mesh,
            in_specs=(
                P("pair", None, "blk"),
                P("pair", "blk"),
                P("pair", None, None),
                P("blk", None),
                P("blk"),
                P("blk"),
                P("pair", None),
            ),
            out_specs=(P("pair", "blk"), P("blk")),
            check_vma=False,
        )(panels, pattern, point_inverse, camera_hessian, damping, camera_grad, point_grad)

    return program
```
